256 devices in a mesh: row: 16 (over y, x), col: 8 (over z), feat: 2 (over core).
Axes of the slice: x: 4, y: 4, z: 8, core: 2. Of those that a mesh axis runs over, the one named last changes fastest.
Arguments:
- fresh: bfloat16 [65536, 512], P(('row', 'col'), 'feat'), may hold values from -6 to 6
- history: bfloat16 [65536, 512], P(('row', 'col'), 'feat'), may hold values from -6 to 6
- adj_val: bfloat16 [16, 8, 256, 128, 128], P('row', 'col'), may hold values from -0.0625 to 0.0625
- tile_row: int32 [16, 8, 256], P('row', 'col'), may hold values from 0 to 31
- tile_col: int32 [16, 8, 256], P('row', 'col'), may hold values from 0 to 63
- tile_count: int32 [16, 8], P('row', 'col'), may hold values from 64 to 256, as said below
- samp_id: int32 [16, 8, 48], P('row', 'col'), may hold values from 0 to 255, as said below
- samp_scale: float32 [16, 8, 48], P('row', 'col'), may hold values from 1 to 4
- weight: bfloat16 [512, 512], P('feat'), may hold values from -0.25 to 0.25
- d_out: bfloat16 [65536, 512], P(('row', 'col'), 'feat'), may hold values from -6 to 6
Outputs:
- layer_out: bfloat16 [65536, 512], P(('row', 'col'), 'feat')
- weight_grad: float32 [512, 512], P('feat')
- fresh_grad: float32 [65536, 512], P(('row', 'col'), 'feat')
The draws below stay inside these ranges and needn't reach their ends.
Inputs may be any that keep to these rules, and one draw needn't show every extreme that they name: `tile_count`: at least a quarter of 256; some device has exactly 256; slots from this count on are ignored. `samp_id`: each is below its own device's tile_count; the largest slot and the first slot are each sampled somewhere.
All inputs are finite; a program needn't handle non-finite values.
Results may differ from the reference program's by a relative error of at most 0.015.
Values may be sent and summed in bfloat16 or wider, within the bound.
No kernel may reach another device: no remote copies, remote signals or barrier semaphores. Data moves between devices by JAX's collectives and lax.ppermute only.
A program may use at most 128 MiB of HBM per device.

```python
import math
import jax
import jax.numpy as jnp
from jax import lax

D = 512
BLK = 128
ROWS_DEV = 512
TILES_DEV = 256
SAMP_DEV = 48
ROW_BLOCKS = 32
COL_BLOCKS = 64
NODES = 65536
N_ROW = 16
N_COL = 8


def live_counts(key):
    key = jax.random.fold_in(key, 101)
    first, second = jax.random.split(key)
    counts = jax.random.randint(first, (N_ROW * N_COL,), TILES_DEV // 4, TILES_DEV + 1)
    place = jax.random.randint(second, (), 0, N_ROW * N_COL)
    counts = counts.at[place].set(TILES_DEV)
    return (counts.reshape(N_ROW, N_COL).astype(jnp.int32), place)


def draw_tile_count(key, part):
    counts, place = live_counts(key)
    return counts


def draw_samp_id(key, part):
    counts, place = live_counts(key)
    key = jax.random.fold_in(key, 7)
    raw = jax.random.randint(key, (N_ROW, N_COL, SAMP_DEV), 0, 1048576)
    slots = (raw % counts[:, :, None]).astype(jnp.int32).reshape(N_ROW * N_COL, SAMP_DEV)
    slots = slots.at[place, 0].set(TILES_DEV - 1)
    slots = slots.at[place, 1].set(0)
    return slots.reshape(N_ROW, N_COL, SAMP_DEV).astype(jnp.int32)


def set_ends(values, stream_key, least, high):
    index_at = [jax.random.randint(jax.random.fold_in(stream_key, axis), (), 0, length) for axis, length in enumerate(values.shape)]
    widest = values.shape.index(max(values.shape))
    beside = index_at[:widest] + [(index_at[widest] + 1) % values.shape[widest]] + index_at[widest + 1:]
    return values.at[tuple(index_at)].set(least).at[tuple(beside)].set(high)


def level_of(own_key, shape, shards, least, top_value):
    def one(axis_at, blocks):
        heights = jax.random.uniform(jax.random.fold_in(jax.random.fold_in(own_key, 6), axis_at), (blocks,), jnp.float32, least / len(shards), top_value / len(shards))
        return jnp.repeat(jnp.exp(heights), shape[axis_at] // blocks).reshape((-1,) + (1,) * (len(shape) - axis_at - 1))

    loudness = one(*shards[0])
    for cut in shards[1:]:
        loudness = loudness * one(*cut)
    return loudness


def bell_draw(stream_key, extent, deviation, reach, cuts=(), held_as=jnp.bfloat16):
    factor_of = level_of(stream_key, extent, cuts, -0.22, 0.18) if cuts else 1.0
    array = jax.random.normal(stream_key, extent, jnp.float32) * deviation * factor_of
    return jnp.minimum(jnp.maximum(array, -reach), reach).astype(held_as)


def setup_inputs(seed: int = 0) -> dict:
    streams_of = jax.random.split(jax.random.key(seed), 11)
    return {
        "fresh": bell_draw(streams_of[0], (NODES, D), 1.0, 6.0, ((0, 128), (1, 2))),
        "history": bell_draw(streams_of[1], (NODES, D), 1.0, 6.0, ((0, 128), (1, 2))),
        "adj_val": bell_draw(streams_of[2], (N_ROW, N_COL, TILES_DEV, BLK, BLK), (BLK * BLK * TILES_DEV // ROWS_DEV) ** -0.5, 0.0625, ((0, 16), (1, 8))),
        "tile_row": set_ends(jax.random.randint(streams_of[3], (N_ROW, N_COL, TILES_DEV), 0, ROW_BLOCKS), jax.random.fold_in(streams_of[3], 1), 0, ROW_BLOCKS - 1).astype(jnp.int32),
        "tile_col": set_ends(jax.random.randint(streams_of[4], (N_ROW, N_COL, TILES_DEV), 0, COL_BLOCKS), jax.random.fold_in(streams_of[4], 1), 0, COL_BLOCKS - 1).astype(jnp.int32),
        "tile_count": draw_tile_count(jax.random.fold_in(streams_of[10], 71), 0),
        "samp_id": draw_samp_id(jax.random.fold_in(streams_of[10], 71), 0),
        "samp_scale": jnp.clip(jnp.exp(math.log(4.0) - 1.3862944 * jax.random.uniform(streams_of[7], (N_ROW, N_COL, SAMP_DEV), jnp.float32) ** level_of(streams_of[7], (N_ROW, N_COL, SAMP_DEV), ((0, 16), (1, 8)), -0.2, 0.2)), 1.0, 4.0),
        "weight": bell_draw(streams_of[8], (D, D), D ** -0.5, 0.25, ((0, 2),)),
        "d_out": bell_draw(streams_of[9], (NODES, D), 1.0, 6.0, ((0, 128), (1, 2))),
    }


def gelu_tanh(value):
    return jax.nn.gelu(value, approximate=True)

def reference(fresh, history, adj_val, tile_row, tile_col, tile_count, samp_id, samp_scale, weight, d_out):
    high = lax.Precision.HIGHEST
    diff = (fresh.astype(jnp.float32) - history.astype(jnp.float32)).astype(jnp.bfloat16)
    hist_sets = history.reshape(N_ROW, N_COL, ROWS_DEV, D)
    diff_sets = diff.reshape(N_ROW, N_COL, ROWS_DEV, D)
    row_range = jnp.arange(ROW_BLOCKS, dtype=jnp.int32)
    col_range = jnp.arange(COL_BLOCKS, dtype=jnp.int32)

    def column_blocks(sets, index):
        picked = lax.dynamic_index_in_dim(sets, index, 1, keepdims=False)
        return picked.reshape(COL_BLOCKS, BLK, D)

    def forward_term(rindex, cindex):
        values = adj_val[rindex, cindex].astype(jnp.float32)
        rows = tile_row[rindex, cindex]
        cols = tile_col[rindex, cindex]
        live = (jnp.arange(TILES_DEV, dtype=jnp.int32) < tile_count[rindex, cindex]).astype(jnp.float32)
        inputs = column_blocks(hist_sets, cindex)[cols].astype(jnp.float32)
        product = jnp.einsum('tij,tjd->tid', values, inputs, precision=high) * live[:, None, None]
        hot = (rows[:, None] == row_range[None, :]).astype(jnp.float32)
        total = jnp.einsum('tb,tid->bid', hot, product, precision=high)
        chosen = samp_id[rindex, cindex]
        sampled = values[chosen]
        sdiff = column_blocks(diff_sets, cindex)[cols[chosen]].astype(jnp.float32)
        sproduct = jnp.einsum('tij,tjd->tid', sampled, sdiff, precision=high) * samp_scale[rindex, cindex][:, None, None]
        shot = (rows[chosen][:, None] == row_range[None, :]).astype(jnp.float32)
        total = total + jnp.einsum('tb,tid->bid', shot, sproduct, precision=high)
        return total.reshape(ROW_BLOCKS * BLK, D)

    def row_set(rindex):

        def add_term(carry, cindex):
            return (carry + forward_term(rindex, cindex), None)
        start = jnp.zeros((ROW_BLOCKS * BLK, D), jnp.float32)
        total, unused = lax.scan(add_term, start, jnp.arange(N_COL, dtype=jnp.int32))
        return total
    zsum = lax.map(row_set, jnp.arange(N_ROW, dtype=jnp.int32)).reshape(NODES, D)
    zval = zsum.astype(jnp.bfloat16)
    pre = jnp.dot(zval, weight, preferred_element_type=jnp.float32)
    layer_out, pull = jax.vjp(gelu_tanh, pre)
    grad_pre = pull(d_out.astype(jnp.float32))[0].astype(jnp.bfloat16)
    weight_grad = jnp.dot(zval.T, grad_pre, preferred_element_type=jnp.float32)
    dz_val = jnp.dot(grad_pre, weight.T, preferred_element_type=jnp.float32).astype(jnp.bfloat16)
    dz_sets = dz_val.reshape(N_ROW, ROW_BLOCKS, BLK, D)

    def backward_term(rindex, cindex):
        chosen = samp_id[rindex, cindex]
        sampled = adj_val[rindex, cindex][chosen].astype(jnp.float32)
        rows = tile_row[rindex, cindex][chosen]
        cols = tile_col[rindex, cindex][chosen]
        grads = dz_sets[rindex][rows].astype(jnp.float32)
        product = jnp.einsum('tji,tjd->tid', sampled, grads, precision=high) * samp_scale[rindex, cindex][:, None, None]
        hot = (cols[:, None] == col_range[None, :]).astype(jnp.float32)
        return jnp.einsum('tb,tid->bid', hot, product, precision=high).reshape(COL_BLOCKS * BLK, D)

    def col_set(cindex):

        def add_term(carry, rindex):
            return (carry + backward_term(rindex, cindex), None)
        start = jnp.zeros((COL_BLOCKS * BLK, D), jnp.float32)
        total, unused = lax.scan(add_term, start, jnp.arange(N_ROW, dtype=jnp.int32))
        return total
    dh_sets = lax.map(col_set, jnp.arange(N_COL, dtype=jnp.int32))
    fresh_grad = dh_sets.reshape(N_COL, N_ROW, ROWS_DEV, D).transpose(1, 0, 2, 3).reshape(NODES, D)
    return (layer_out.astype(jnp.bfloat16), weight_grad, fresh_grad)
```

```python
import functools
import jax
import jax.numpy as jnp
from jax import lax
from jax.experimental import pallas as pl
from jax.experimental.pallas import tpu as pltpu
from jax.sharding import Mesh, PartitionSpec as P

BF = jnp.bfloat16
F32 = jnp.float32
GROUP = 8
CHUNKS = 8
VMEM = pl.BlockSpec(memory_space=pltpu.VMEM)
HBM = pl.BlockSpec(memory_space=pl.ANY)
SMEM = pl.BlockSpec(memory_space=pltpu.SMEM)


def shift(x, axis, step):
    n = lax.axis_size(axis)
    return lax.ppermute(x, axis, [(i, (i + step) % n) for i in range(n)])


def gather_two(x, first, second):
    group = jnp.concatenate(
        [x, shift(x, first, -1), shift(x, first, 2), shift(x, first, 1)], axis=0
    )
    below = shift(group, second, 1)
    above = shift(group, second, -1)
    half = group.shape[0] // 2
    far_lo = shift(below[:half], second, 1)
    far_hi = shift(above[half:], second, -1)
    return group, above, far_lo, far_hi, below


def gather_copies(parts, dst, sems, base):
    copies = []
    at = 0
    for n, part in enumerate(parts):
        size = part.shape[0]
        copies.append(pltpu.make_async_copy(part, dst.at[pl.ds(at, size)], sems.at[base + n]))
        at += size
    return copies


def forward_kernel(
    rows, cols, srow, scol, sid, meta, scale, adj,
    h0, h1, h2, h3, h4, d0, d1, d2, d3, d4,
    o4a, o4b, o3, o2, o1, o0, m1, m2, m3,
    tiles, hist, diff, acc, sems,
):
    count = meta[0]
    zpos = meta[1]
    nodes = gather_copies((h0, h1, h2, h3, h4), hist, sems, 0)
    nodes += gather_copies((d0, d1, d2, d3, d4), diff, sems, 5)
    per = tiles.shape[0] // CHUNKS
    loads = [
        pltpu.make_async_copy(
            adj.at[pl.ds(c * per, per)], tiles.at[pl.ds(c * per, per)], sems.at[10 + c]
        )
        for c in range(CHUNKS)
    ]
    for copy in nodes[:5]:
        copy.start()
    for copy in loads:
        copy.start()
    for copy in nodes[5:]:
        copy.start()
    acc[...] = jnp.zeros_like(acc)
    for copy in nodes[:5]:
        copy.wait()
    groups = (count + GROUP - 1) // GROUP
    each = per // GROUP

    for c in range(CHUNKS):
        loads[c].wait()

        def body(g, carry):
            start = g * GROUP
            products = [
                jnp.dot(tiles[start + u], hist[cols[start + u]], preferred_element_type=F32)
                for u in range(GROUP)
            ]
            for u in range(GROUP):
                r = rows[start + u]
                acc[r] = acc[r] + products[u]
            return carry

        lax.fori_loop(c * each, jnp.clip(groups, c * each, (c + 1) * each), body, 0)
    for copy in nodes[5:]:
        copy.wait()

    def sampled(g, carry):
        start = g * GROUP
        products = [
            jnp.dot(
                tiles[sid[start + u]], diff[scol[start + u]], preferred_element_type=F32
            )
            * scale[start + u]
            for u in range(GROUP)
        ]
        for u in range(GROUP):
            r = srow[start + u]
            acc[r] = acc[r] + products[u]
        return carry

    lax.fori_loop(0, sid.shape[0] // GROUP, sampled, 0)

    def put(out, k, lo, size):
        start = lax.rem(zpos + k, 8) * 4 + lo
        out[...] = acc[pl.ds(start, size)].astype(out.dtype)

    put(o4a, 4, 0, 2)
    put(o4b, 4, 2, 2)
    for out, k in ((o3, 3), (o2, 2), (o1, 1), (o0, 0), (m1, 7), (m2, 6), (m3, 5)):
        put(out, k, 0, 4)


def forward_tiles(rows, cols, srow, scol, sid, meta, scale, adj, hist, diff):
    n_tiles, blk, _ = adj.shape
    half = hist[0].shape[-1]
    whole = jax.ShapeDtypeStruct((4, blk, half), BF)
    part = jax.ShapeDtypeStruct((2, blk, half), BF)
    return pl.pallas_call(
        forward_kernel,
        out_shape=[part, part, whole, whole, whole, whole, whole, whole, whole],
        in_specs=[SMEM] * 7 + [HBM] * 11,
        out_specs=[VMEM] * 9,
        scratch_shapes=[
            pltpu.VMEM((n_tiles, blk, blk), BF),
            pltpu.VMEM((64, blk, half), BF),
            pltpu.VMEM((64, blk, half), BF),
            pltpu.VMEM((33, blk, half), F32),
            pltpu.SemaphoreType.DMA((10 + CHUNKS,)),
        ],
        compiler_params=pltpu.CompilerParams(vmem_limit_bytes=48 * 1024 * 1024),
        cost_estimate=pl.CostEstimate(
            flops=2 * 304 * blk * blk * half, bytes_accessed=20 << 20, transcendentals=0
        ),
        name="forward_tiles",
    )(rows, cols, srow, scol, sid, meta, scale, adj, *hist, *diff)


def backward_kernel(
    srow, scol, sid, scale, adj, z0, z1, z2, z3, z4, z5, z6, z7, z8,
    out, tiles, grads, acc, sems,
):
    copies = gather_copies((z0, z1, z2, z3, z4, z5, z6, z7, z8), grads, sems, 0)
    for copy in copies:
        copy.start()
    n = sid.shape[0]

    def fetch(s):
        return pltpu.make_async_copy(adj.at[sid[s]], tiles.at[s], sems.at[9 + s])

    def begin(s, carry):
        fetch(s).start()
        return carry

    lax.fori_loop(0, n, begin, 0)
    acc[...] = jnp.zeros_like(acc)
    for copy in copies:
        copy.wait()

    def finish(s, carry):
        fetch(s).wait()
        return carry

    lax.fori_loop(0, n, finish, 0)

    def body(g, carry):
        start = g * GROUP
        products = [
            lax.dot_general(
                tiles[start + u],
                grads[srow[start + u]],
                (((0,), (0,)), ((), ())),
                preferred_element_type=F32,
            )
            * scale[start + u]
            for u in range(GROUP)
        ]
        for u in range(GROUP):
            c = scol[start + u]
            acc[c] = acc[c] + products[u]
        return carry

    lax.fori_loop(0, n // GROUP, body, 0)
    out[...] = acc[...].astype(out.dtype)


def backward_tiles(srow, scol, sid, scale, adj, parts):
    _, blk, _ = adj.shape
    half = parts[0].shape[-1]
    n = sid.shape[0]
    return pl.pallas_call(
        backward_kernel,
        out_shape=jax.ShapeDtypeStruct((64, blk, half), BF),
        in_specs=[SMEM] * 4 + [HBM] * 10,
        out_specs=VMEM,
        scratch_shapes=[
            pltpu.VMEM((n, blk, blk), BF),
            pltpu.VMEM((32, blk, half), BF),
            pltpu.VMEM((64, blk, half), F32),
            pltpu.SemaphoreType.DMA((9 + n,)),
        ],
        compiler_params=pltpu.CompilerParams(vmem_limit_bytes=32 * 1024 * 1024),
        cost_estimate=pl.CostEstimate(
            flops=2 * n * blk * blk * half, bytes_accessed=8 << 20, transcendentals=0
        ),
        name="backward_tiles",
    )(srow, scol, sid, scale, adj, *parts)


def dense_kernel(z, zo, w, wo, d, do, out, dz, wg):
    half = d.shape[1]
    zv = z[...]
    pre = jnp.dot(zv, w[...], preferred_element_type=F32)
    pre += jnp.dot(zo[...], wo[...], preferred_element_type=F32)
    inner = 0.7978845608 * (pre + 0.044715 * pre * pre * pre)
    th = jnp.tanh(inner)
    cdf = 0.5 * (1.0 + th)
    out[...] = (pre * cdf)[:, :half].astype(out.dtype)
    slope = cdf + 0.5 * pre * (1.0 - th * th) * (
        0.7978845608 * (1.0 + 3.0 * 0.044715 * pre * pre)
    )
    cot = jnp.concatenate([d[...], do[...]], axis=1).astype(F32)
    g = (cot * slope).astype(BF)
    dz[...] = lax.dot_general(
        g, w[...], (((1,), (1,)), ((), ())), preferred_element_type=F32
    ).astype(BF)
    wg[...] = lax.dot_general(
        zv, g, (((0,), (0,)), ((), ())), preferred_element_type=F32
    ).astype(wg.dtype)


def dense(z, zo, w, wo, d, do):
    rows, half = z.shape
    return pl.pallas_call(
        dense_kernel,
        out_shape=[
            jax.ShapeDtypeStruct((rows, half), BF),
            jax.ShapeDtypeStruct((rows, half), BF),
            jax.ShapeDtypeStruct(w.shape, BF),
        ],
        in_specs=[VMEM] * 6,
        out_specs=[VMEM] * 3,
        compiler_params=pltpu.CompilerParams(vmem_limit_bytes=32 * 1024 * 1024),
        cost_estimate=pl.CostEstimate(
            flops=8 * rows * half * 2 * half, bytes_accessed=2 << 20, transcendentals=rows * half * 2
        ),
        name="dense",
    )(z, zo, w, wo, d, do)


def plus(a, b):
    return (a.astype(F32) + b.astype(F32)).astype(BF)


def gather_ring(x):
    blocks = {0: x}
    up = down = x
    for k in (1, 2, 3):
        up, down = shift(up, "z", 1), shift(down, "z", -1)
        blocks[8 - k], blocks[k] = up, down
    half = x.shape[0] // 2
    far_lo = shift(up[:half], "z", 1)
    far_hi = shift(down[half:], "z", -1)
    return [blocks[0], blocks[1], blocks[2], blocks[3], far_lo, far_hi, blocks[5], blocks[6], blocks[7]]


def local(
    fresh, history, adj_val, tile_row, tile_col, tile_count, samp_id, samp_scale, weight, d_out
):
    adj = adj_val[0, 0]
    rows = tile_row[0, 0]
    cols = tile_col[0, 0]
    count = tile_count[0, 0]
    sid = samp_id[0, 0]
    scale = samp_scale[0, 0]
    n_tiles, blk, _ = adj.shape
    half = fresh.shape[1]
    xpos, ypos, zpos = lax.axis_index("x"), lax.axis_index("y"), lax.axis_index("z")
    core = lax.axis_index("core")
    hist_in = history.reshape(4, blk, half)
    diff_in = (fresh.astype(F32) - history.astype(F32)).astype(BF).reshape(4, blk, half)
    hist = gather_two(hist_in, "x", "y")
    diff = gather_two(diff_in, "y", "x")

    xrel = (cols // 4 - xpos) % 4
    yrel = (cols // 16 - ypos) % 4
    hcol = (yrel * 4 + xrel) * 4 + cols % 4
    dcol = (xrel * 4 + yrel) * 4 + cols % 4
    live_row = jnp.where(jnp.arange(n_tiles, dtype=jnp.int32) < count, rows, 32)
    srow = rows[sid]
    meta = jnp.stack([count, zpos.astype(jnp.int32)])
    o4a, o4b, o3, o2, o1, o0, m1, m2, m3 = forward_tiles(
        live_row, hcol, srow, dcol[sid], sid, meta, scale, adj, hist, diff
    )

    up, down = shift(o4a, "z", 1), shift(o4b, "z", -1)
    up = shift(jnp.concatenate([plus(up, o3[:2]), o3[2:]], axis=0), "z", 1)
    down = shift(jnp.concatenate([m3[:2], plus(down, m3[2:])], axis=0), "z", -1)
    up, down = shift(plus(up, o2), "z", 1), shift(plus(down, m2), "z", -1)
    up, down = shift(plus(up, o1), "z", 1), shift(plus(down, m1), "z", -1)
    zval = (up.astype(F32) + down.astype(F32) + o0.astype(F32)).astype(BF)
    zval = zval.reshape(4 * blk, half)

    wrel = jnp.where(core == 0, weight, jnp.roll(weight, half, axis=1))
    wother = shift(weight, "core", 1)
    wother = jnp.where(core == 0, wother, jnp.roll(wother, half, axis=1))
    d_other = shift(d_out, "core", 1)
    zother = shift(zval, "core", 1)
    layer_out, dz, wpart = dense(zval, zother, wrel, wother, d_out, d_other)

    parts = gather_ring(dz.reshape(4, blk, half))
    row_rel = ((srow // 4 - zpos) % 8) * 4 + srow % 4
    back = backward_tiles(row_rel, cols[sid], sid, scale, adj, parts)
    back = lax.all_to_all(back, ("y", "x"), 0, 0, tiled=True)
    fresh_grad = back.reshape(16, 4 * blk, half).astype(F32).sum(0)

    wide = weight.shape[1]
    wparts = lax.all_to_all(wpart, "z", 0, 0, tiled=True)
    wsum = wparts.reshape(8, half // 8, wide).astype(F32).sum(0).astype(BF)
    wparts = lax.all_to_all(
        jnp.broadcast_to(wsum, (16,) + wsum.shape), ("y", "x"), 0, 0, tiled=True
    )
    wsum = wparts.astype(F32).sum(0).astype(BF)
    wgrad = lax.all_to_all(
        jnp.broadcast_to(wsum, (8,) + wsum.shape), "z", 0, 0, tiled=True
    )
    wgrad = wgrad.reshape(half, wide).astype(F32)
    wgrad = jnp.where(core == 0, wgrad, jnp.roll(wgrad, half, axis=1))
    return layer_out, wgrad, fresh_grad


def solution(mesh):
    fine = Mesh(mesh.devices.reshape(4, 4, 8, 2), ("y", "x", "z", "core"))
    row = ("y", "x")
    nodes = P(("y", "x", "z"), "core")
    placed = (
        nodes,
        nodes,
        P(row, "z", None, None, None),
        P(row, "z", None),
        P(row, "z", None),
        P(row, "z"),
        P(row, "z", None),
        P(row, "z", None),
        P("core", None),
        nodes,
    )
    return jax.shard_map(
        local,
        mesh=fine,
        in_specs=placed,
        out_specs=(nodes, P("core", None), nodes),
        check_vma=False,
    )
```

```python
import functools
import jax
import jax.numpy as jnp
from jax import lax
from jax.experimental import pallas as pl
from jax.experimental.pallas import tpu as pltpu
from jax.sharding import Mesh, PartitionSpec as P

BF = jnp.bfloat16
F32 = jnp.float32
GROUP = 8
PARTS = 8
VMEM = pl.BlockSpec(memory_space=pltpu.VMEM)
HBM = pl.BlockSpec(memory_space=pl.ANY)
SMEM = pl.BlockSpec(memory_space=pltpu.SMEM)


def shift(x, axis, step):
    n = lax.axis_size(axis)
    return lax.ppermute(x, axis, [(i, (i + step) % n) for i in range(n)])


def join(a, b):
    return jnp.concatenate([a, b], axis=0)


def gather_both(one, two, adj):
    axes = (("x", "y"), ("y", "x"))
    own = (one, two)
    next_ = [shift(v, a, -1) for v, (a, _) in zip(own, axes)]
    prev = [shift(v, a, 1) for v, (a, _) in zip(own, axes)]
    one, two, next_[0], next_[1] = lax.optimization_barrier((one, two, next_[0], next_[1]))
    far = [shift(v, a, 2) for v, (a, _) in zip((one, two), axes)]
    low = [join(v, n) for v, n in zip((one, two), next_)]
    low[0], low[1], prev[0], prev[1] = lax.optimization_barrier((low[0], low[1], prev[0], prev[1]))
    high = [join(f, p) for f, p in zip(far, prev)]
    below_low = [shift(v, b, 1) for v, (_, b) in zip(low, axes)]
    above_low = [shift(v, b, -1) for v, (_, b) in zip(low, axes)]
    high[0], high[1], below_low[0], below_low[1], adj = lax.optimization_barrier(
        (high[0], high[1], below_low[0], below_low[1], adj)
    )
    tiles = load_tiles(adj)
    below_high = [shift(v, b, 1) for v, (_, b) in zip(high, axes)]
    above_high = [shift(v, b, -1) for v, (_, b) in zip(high, axes)]
    far_low = [shift(v, b, 1) for v, (_, b) in zip(below_low, axes)]
    far_high = [shift(v, b, -1) for v, (_, b) in zip(above_high, axes)]
    return [
        (low[n], high[n], above_low[n], above_high[n], far_low[n], far_high[n], below_low[n], below_high[n])
        for n in range(2)
    ] + [tiles]


def gather_copies(parts, dst, sems, base):
    copies = []
    at = 0
    for n, part in enumerate(parts):
        size = part.shape[0]
        copies.append(pltpu.make_async_copy(part, dst.at[pl.ds(at, size)], sems.at[base + n]))
        at += size
    return copies


def load_kernel(src, dst):
    def move(sem):
        copy = pltpu.make_async_copy(src, dst, sem)
        copy.start()
        copy.wait()

    pl.run_scoped(move, pltpu.SemaphoreType.DMA)


def load_tiles(adj):
    return pl.pallas_call(
        load_kernel,
        out_shape=jax.ShapeDtypeStruct(adj.shape, adj.dtype),
        in_specs=[HBM],
        out_specs=VMEM,
        compiler_params=pltpu.CompilerParams(vmem_limit_bytes=16 * 1024 * 1024),
        cost_estimate=pl.CostEstimate(flops=0, bytes_accessed=8 << 20, transcendentals=0),
        name="load_tiles",
    )(adj)


def forward_kernel(rows, cols, srow, scol, sid, meta, scale, tiles, *refs):
    parts, rest = refs[: 2 * PARTS], refs[2 * PARTS :]
    o4a, o4b, o3, o2, o1, o0, m1, m2, m3, chosen = rest[:10]
    hist, diff, acc, sems = rest[10:]
    count = meta[0]
    zpos = meta[1]
    nodes = gather_copies(parts[:PARTS], hist, sems, 0)
    nodes += gather_copies(parts[PARTS:], diff, sems, PARTS)
    for copy in nodes[:PARTS]:
        copy.start()
    for copy in nodes[PARTS:]:
        copy.start()
    acc[...] = jnp.zeros_like(acc)
    for copy in nodes[:PARTS]:
        copy.wait()
    groups = (count + GROUP - 1) // GROUP

    def body(g, carry):
        start = g * GROUP
        products = [
            jnp.dot(tiles[start + u], hist[cols[start + u]], preferred_element_type=F32)
            for u in range(GROUP)
        ]
        for u in range(GROUP):
            r = rows[start + u]
            acc[r] = acc[r] + products[u]
        return carry

    lax.fori_loop(0, groups, body, 0)
    for copy in nodes[PARTS:]:
        copy.wait()

    def sampled(g, carry):
        start = g * GROUP
        for u in range(GROUP):
            chosen[start + u] = tiles[sid[start + u]]
        products = [
            jnp.dot(
                tiles[sid[start + u]], diff[scol[start + u]], preferred_element_type=F32
            )
            * scale[start + u]
            for u in range(GROUP)
        ]
        for u in range(GROUP):
            r = srow[start + u]
            acc[r] = acc[r] + products[u]
        return carry

    lax.fori_loop(0, sid.shape[0] // GROUP, sampled, 0)

    def put(out, k, lo, size):
        start = lax.rem(zpos + k, 8) * 4 + lo
        out[...] = acc[pl.ds(start, size)].astype(out.dtype)

    put(o4a, 4, 0, 2)
    put(o4b, 4, 2, 2)
    for out, k in ((o3, 3), (o2, 2), (o1, 1), (o0, 0), (m1, 7), (m2, 6), (m3, 5)):
        put(out, k, 0, 4)


def forward_tiles(rows, cols, srow, scol, sid, meta, scale, adj, hist, diff):
    n_tiles, blk, _ = adj.shape
    half = hist[0].shape[-1]
    whole = jax.ShapeDtypeStruct((4, blk, half), BF)
    part = jax.ShapeDtypeStruct((2, blk, half), BF)
    chosen = jax.ShapeDtypeStruct((sid.shape[0], blk, blk), BF)
    return pl.pallas_call(
        forward_kernel,
        out_shape=[part, part] + [whole] * 7 + [chosen],
        in_specs=[SMEM] * 7 + [VMEM] + [HBM] * (2 * PARTS),
        out_specs=[VMEM] * 10,
        scratch_shapes=[
            pltpu.VMEM((64, blk, half), BF),
            pltpu.VMEM((64, blk, half), BF),
            pltpu.VMEM((33, blk, half), F32),
            pltpu.SemaphoreType.DMA((2 * PARTS,)),
        ],
        compiler_params=pltpu.CompilerParams(vmem_limit_bytes=26 * 1024 * 1024),
        cost_estimate=pl.CostEstimate(
            flops=2 * 304 * blk * blk * half, bytes_accessed=20 << 20, transcendentals=0
        ),
        name="forward_tiles",
    )(rows, cols, srow, scol, sid, meta, scale, adj, *hist, *diff)


def backward_kernel(srow, scol, meta, scale, tiles, *refs):
    parts, outs = refs[:9], refs[9:17]
    grads, acc, sems = refs[17:]
    copies = gather_copies(parts, grads, sems, 0)
    for copy in copies:
        copy.start()
    acc[...] = jnp.zeros_like(acc)
    for copy in copies:
        copy.wait()

    def body(g, carry):
        start = g * GROUP
        products = [
            lax.dot_general(
                tiles[start + u],
                grads[srow[start + u]],
                (((0,), (0,)), ((), ())),
                preferred_element_type=F32,
            )
            * scale[start + u]
            for u in range(GROUP)
        ]
        for u in range(GROUP):
            c = scol[start + u]
            acc[c] = acc[c] + products[u]
        return carry

    lax.fori_loop(0, tiles.shape[0] // GROUP, body, 0)
    xpos, ypos = meta[2], meta[3]
    lanes = acc.shape[2] // 2
    for k in range(4):
        for j in range(4):
            at = (lax.rem(ypos + j, 4) * 4 + lax.rem(xpos + k, 4)) * 4
            block = acc[pl.ds(at, 4)]
            outs[k][4 * j : 4 * j + 4] = block[:, :, :lanes].astype(BF)
            outs[4 + j][4 * k : 4 * k + 4] = block[:, :, lanes:].astype(BF)


def backward_tiles(srow, scol, meta, scale, chosen, parts):
    n, blk, _ = chosen.shape
    half = parts[0].shape[-1]
    return pl.pallas_call(
        backward_kernel,
        out_shape=[jax.ShapeDtypeStruct((16, blk, half // 2), BF)] * 8,
        in_specs=[SMEM] * 4 + [VMEM] + [HBM] * 9,
        out_specs=[VMEM] * 8,
        scratch_shapes=[
            pltpu.VMEM((32, blk, half), BF),
            pltpu.VMEM((64, blk, half), F32),
            pltpu.SemaphoreType.DMA((9,)),
        ],
        compiler_params=pltpu.CompilerParams(vmem_limit_bytes=60 * 1024 * 1024),
        cost_estimate=pl.CostEstimate(
            flops=2 * n * blk * blk * half, bytes_accessed=8 << 20, transcendentals=0
        ),
        name="backward_tiles",
    )(srow, scol, meta, scale, chosen, *parts)


def scatter_both(left, right, rider):
    axes = (("x", "y"), ("y", "x"))
    both = (left, right)
    one = [shift(p[1], a, 1) for p, (a, _) in zip(both, axes)]
    three = [shift(p[3], a, -1) for p, (a, _) in zip(both, axes)]
    two = [left[2], right[2]]
    one[0], one[1], two[0], two[1], rider = lax.optimization_barrier(
        (one[0], one[1], two[0], two[1], rider)
    )
    two = [shift(t, a, 2) for t, (a, _) in zip(two, axes)]
    total = [
        p[0].astype(F32) + i.astype(F32) + t.astype(F32) + m.astype(F32)
        for p, i, t, m in zip(both, one, three, two)
    ]
    out = []
    for t, (_, b) in zip(total, axes):
        send = [t[4 * j : 4 * j + 4].astype(BF) for j in (1, 2, 3)]
        got = [shift(p, b, j if j < 3 else -1) for j, p in zip((1, 2, 3), send)]
        out.append(t[:4] + sum(p.astype(F32) for p in got))
    return jnp.concatenate(out, axis=2), rider


def dense_kernel(core, z, zo, w, wo, d, do, out, dz, wg):
    half = d.shape[1]
    first = core[0] == 0
    zv = z[...]
    pre = jnp.dot(zv, w[...], preferred_element_type=F32)
    pre += jnp.dot(zo[...], wo[...], preferred_element_type=F32)
    inner = 0.7978845608 * (pre + 0.044715 * pre * pre * pre)
    th = jnp.tanh(inner)
    cdf = 0.5 * (1.0 + th)
    act = pre * cdf
    out[...] = jnp.where(first, act[:, :half], act[:, half:]).astype(out.dtype)
    slope = cdf + 0.5 * pre * (1.0 - th * th) * (
        0.7978845608 * (1.0 + 3.0 * 0.044715 * pre * pre)
    )
    mine, other = d[...].astype(F32), do[...].astype(F32)
    cot = jnp.concatenate(
        [jnp.where(first, mine, other), jnp.where(first, other, mine)], axis=1
    )
    g = (cot * slope).astype(BF)
    dz[...] = lax.dot_general(
        g, w[...], (((1,), (1,)), ((), ())), preferred_element_type=F32
    ).astype(BF)
    wg[...] = lax.dot_general(
        zv, g, (((0,), (0,)), ((), ())), preferred_element_type=F32
    ).astype(wg.dtype)


def dense(core, z, zo, w, wo, d, do):
    rows, half = z.shape
    return pl.pallas_call(
        dense_kernel,
        out_shape=[
            jax.ShapeDtypeStruct((rows, half), BF),
            jax.ShapeDtypeStruct((rows, half), BF),
            jax.ShapeDtypeStruct(w.shape, F32),
        ],
        in_specs=[SMEM] + [VMEM] * 6,
        out_specs=[VMEM] * 3,
        compiler_params=pltpu.CompilerParams(vmem_limit_bytes=32 * 1024 * 1024),
        cost_estimate=pl.CostEstimate(
            flops=8 * rows * half * 2 * half, bytes_accessed=2 << 20, transcendentals=rows * half * 2
        ),
        name="dense",
    )(core, z, zo, w, wo, d, do)


def plus(a, b):
    return (a.astype(F32) + b.astype(F32)).astype(BF)


def gather_ring(x):
    blocks = {0: x}
    up = down = x
    for k in (1, 2, 3):
        up, down = shift(up, "z", 1), shift(down, "z", -1)
        blocks[8 - k], blocks[k] = up, down
    half = x.shape[0] // 2
    far_lo = shift(up[:half], "z", 1)
    far_hi = shift(down[half:], "z", -1)
    return [blocks[0], blocks[1], blocks[2], blocks[3], far_lo, far_hi, blocks[5], blocks[6], blocks[7]]


def local(
    fresh, history, adj_val, tile_row, tile_col, tile_count, samp_id, samp_scale, weight, d_out
):
    adj = adj_val[0, 0]
    rows = tile_row[0, 0]
    cols = tile_col[0, 0]
    count = tile_count[0, 0]
    sid = samp_id[0, 0]
    scale = samp_scale[0, 0]
    n_tiles, blk, _ = adj.shape
    half = fresh.shape[1]
    xpos, ypos, zpos = lax.axis_index("x"), lax.axis_index("y"), lax.axis_index("z")
    core = lax.axis_index("core")
    hist_in = history.reshape(4, blk, half)
    diff_in = (fresh.astype(F32) - history.astype(F32)).astype(BF).reshape(4, blk, half)
    hist, diff, tiles = gather_both(hist_in, diff_in, adj)

    xrel = (cols // 4 - xpos) % 4
    yrel = (cols // 16 - ypos) % 4
    hcol = (yrel * 4 + xrel) * 4 + cols % 4
    dcol = (xrel * 4 + yrel) * 4 + cols % 4
    live_row = jnp.where(jnp.arange(n_tiles, dtype=jnp.int32) < count, rows, 32)
    srow = rows[sid]
    meta = jnp.stack([count, zpos, xpos, ypos]).astype(jnp.int32)
    o4a, o4b, o3, o2, o1, o0, m1, m2, m3, chosen = forward_tiles(
        live_row, hcol, srow, dcol[sid], sid, meta, scale, tiles, hist, diff
    )

    up, down = shift(o4a, "z", 1), shift(o4b, "z", -1)
    up = shift(jnp.concatenate([plus(up, o3[:2]), o3[2:]], axis=0), "z", 1)
    down = shift(jnp.concatenate([m3[:2], plus(down, m3[2:])], axis=0), "z", -1)
    up, down = shift(plus(up, o2), "z", 1), shift(plus(down, m2), "z", -1)
    up, down = shift(plus(up, o1), "z", 1), shift(plus(down, m1), "z", -1)
    zval = (up.astype(F32) + down.astype(F32) + o0.astype(F32)).astype(BF)
    zval = zval.reshape(4 * blk, half)

    wother = shift(weight, "core", 1)
    d_other = shift(d_out, "core", 1)
    zother = shift(zval, "core", 1)
    layer_out, dz, wpart = dense(
        core.astype(jnp.int32).reshape(1), zval, zother, weight, wother, d_out, d_other
    )

    parts = gather_ring(dz.reshape(4, blk, half))
    row_rel = ((srow // 4 - zpos) % 8) * 4 + srow % 4
    wsum = lax.psum_scatter(wpart, "z", scatter_dimension=0, tiled=True)
    wsum, parts[4], parts[5] = lax.optimization_barrier((wsum, parts[4], parts[5]))
    back = backward_tiles(row_rel, cols[sid], meta, scale, chosen, parts)
    fresh_grad, wsum = scatter_both(back[:4], back[4:], wsum)
    fresh_grad = fresh_grad.reshape(4 * blk, half)
    wsum = wsum.astype(BF)
    wparts = lax.all_to_all(
        jnp.broadcast_to(wsum, (16,) + wsum.shape), ("y", "x"), 0, 0, tiled=True
    )
    wsum = wparts.astype(F32).sum(0).astype(BF)
    wgrad = lax.all_to_all(
        jnp.broadcast_to(wsum, (8,) + wsum.shape), "z", 0, 0, tiled=True
    )
    wgrad = wgrad.reshape(weight.shape).astype(F32)
    return layer_out, wgrad, fresh_grad


def solution(mesh):
    fine = Mesh(mesh.devices.reshape(4, 4, 8, 2), ("y", "x", "z", "core"))
    row = ("y", "x")
    nodes = P(("y", "x", "z"), "core")
    placed = (
        nodes,
        nodes,
        P(row, "z", None, None, None),
        P(row, "z", None),
        P(row, "z", None),
        P(row, "z"),
        P(row, "z", None),
        P(row, "z", None),
        P("core", None),
        nodes,
    )
    return jax.shard_map(
        local,
        mesh=fine,
        in_specs=placed,
        out_specs=(nodes, P("core", None), nodes),
        check_vma=False,
    )
```

```python
import functools
import jax
import jax.numpy as jnp
from jax import lax
from jax.experimental import pallas as pl
from jax.experimental.pallas import tpu as pltpu
from jax.sharding import Mesh, PartitionSpec as P

BF = jnp.bfloat16
F32 = jnp.float32
GROUP = 8
PARTS = 8
VMEM = pl.BlockSpec(memory_space=pltpu.VMEM)
HBM = pl.BlockSpec(memory_space=pl.ANY)
SMEM = pl.BlockSpec(memory_space=pltpu.SMEM)


def shift(x, axis, step):
    n = lax.axis_size(axis)
    return lax.ppermute(x, axis, [(i, (i + step) % n) for i in range(n)])


def join(a, b):
    return jnp.concatenate([a, b], axis=0)


def gather_both(one, two, adj):
    axes = (("x", "y"), ("y", "x"))
    own = (one, two)
    next_ = [shift(v, a, -1) for v, (a, _) in zip(own, axes)]
    prev = [shift(v, a, 1) for v, (a, _) in zip(own, axes)]
    one, two, next_[0], next_[1] = lax.optimization_barrier((one, two, next_[0], next_[1]))
    far = [shift(v, a, 2) for v, (a, _) in zip((one, two), axes)]
    low = [join(v, n) for v, n in zip((one, two), next_)]
    low[0], low[1], prev[0], prev[1] = lax.optimization_barrier((low[0], low[1], prev[0], prev[1]))
    high = [join(f, p) for f, p in zip(far, prev)]
    below_low = [shift(v, b, 1) for v, (_, b) in zip(low, axes)]
    above_low = [shift(v, b, -1) for v, (_, b) in zip(low, axes)]
    high[0], high[1], below_low[0], below_low[1], adj = lax.optimization_barrier(
        (high[0], high[1], below_low[0], below_low[1], adj)
    )
    tiles = load_tiles(adj)
    below_high = [shift(v, b, 1) for v, (_, b) in zip(high, axes)]
    above_high = [shift(v, b, -1) for v, (_, b) in zip(high, axes)]
    far_low = [shift(v, b, 1) for v, (_, b) in zip(below_low, axes)]
    far_high = [shift(v, b, -1) for v, (_, b) in zip(above_high, axes)]
    return [
        (low[n], high[n], above_low[n], above_high[n], far_low[n], far_high[n], below_low[n], below_high[n])
        for n in range(2)
    ] + [tiles]


def gather_copies(parts, dst, sems, base):
    copies = []
    at = 0
    for n, part in enumerate(parts):
        size = part.shape[0]
        copies.append(pltpu.make_async_copy(part, dst.at[pl.ds(at, size)], sems.at[base + n]))
        at += size
    return copies


def load_kernel(src, dst):
    def move(sem):
        copy = pltpu.make_async_copy(src, dst, sem)
        copy.start()
        copy.wait()

    pl.run_scoped(move, pltpu.SemaphoreType.DMA)


def load_tiles(adj):
    return pl.pallas_call(
        load_kernel,
        out_shape=jax.ShapeDtypeStruct(adj.shape, adj.dtype),
        in_specs=[HBM],
        out_specs=VMEM,
        compiler_params=pltpu.CompilerParams(vmem_limit_bytes=16 * 1024 * 1024),
        cost_estimate=pl.CostEstimate(flops=0, bytes_accessed=8 << 20, transcendentals=0),
        name="load_tiles",
    )(adj)


def forward_kernel(rows, cols, srow, scol, sid, meta, scale, tiles, *refs):
    parts, rest = refs[: 2 * PARTS], refs[2 * PARTS :]
    o4a, o4b, o3, o2, o1, o0, m1, m2, m3, chosen = rest[:10]
    hist, diff, acc, sems = rest[10:]
    count = meta[0]
    zpos = meta[1]
    nodes = gather_copies(parts[:PARTS], hist, sems, 0)
    nodes += gather_copies(parts[PARTS:], diff, sems, PARTS)
    for copy in nodes[:PARTS]:
        copy.start()
    for copy in nodes[PARTS:]:
        copy.start()
    acc[...] = jnp.zeros_like(acc)
    for copy in nodes[:PARTS]:
        copy.wait()
    groups = (count + GROUP - 1) // GROUP

    def body(g, carry):
        start = g * GROUP
        products = [
            jnp.dot(tiles[start + u], hist[cols[start + u]], preferred_element_type=F32)
            for u in range(GROUP)
        ]
        for u in range(GROUP):
            r = rows[start + u]
            acc[r] = acc[r] + products[u]
        return carry

    lax.fori_loop(0, groups, body, 0)
    for copy in nodes[PARTS:]:
        copy.wait()

    def sampled(g, carry):
        start = g * GROUP
        for u in range(GROUP):
            chosen[start + u] = tiles[sid[start + u]]
        products = [
            jnp.dot(
                tiles[sid[start + u]], diff[scol[start + u]], preferred_element_type=F32
            )
            * scale[start + u]
            for u in range(GROUP)
        ]
        for u in range(GROUP):
            r = srow[start + u]
            acc[r] = acc[r] + products[u]
        return carry

    lax.fori_loop(0, sid.shape[0] // GROUP, sampled, 0)

    def put(out, k, lo, size):
        start = lax.rem(zpos + k, 8) * 4 + lo
        out[...] = acc[pl.ds(start, size)].astype(out.dtype)

    put(o4a, 4, 0, 2)
    put(o4b, 4, 2, 2)
    for out, k in ((o3, 3), (o2, 2), (o1, 1), (o0, 0), (m1, 7), (m2, 6), (m3, 5)):
        put(out, k, 0, 4)


def forward_tiles(rows, cols, srow, scol, sid, meta, scale, adj, hist, diff):
    n_tiles, blk, _ = adj.shape
    half = hist[0].shape[-1]
    whole = jax.ShapeDtypeStruct((4, blk, half), BF)
    part = jax.ShapeDtypeStruct((2, blk, half), BF)
    chosen = jax.ShapeDtypeStruct((sid.shape[0], blk, blk), BF)
    return pl.pallas_call(
        forward_kernel,
        out_shape=[part, part] + [whole] * 7 + [chosen],
        in_specs=[SMEM] * 7 + [VMEM] + [HBM] * (2 * PARTS),
        out_specs=[VMEM] * 10,
        scratch_shapes=[
            pltpu.VMEM((64, blk, half), BF),
            pltpu.VMEM((64, blk, half), BF),
            pltpu.VMEM((33, blk, half), F32),
            pltpu.SemaphoreType.DMA((2 * PARTS,)),
        ],
        compiler_params=pltpu.CompilerParams(vmem_limit_bytes=26 * 1024 * 1024),
        cost_estimate=pl.CostEstimate(
            flops=2 * 304 * blk * blk * half, bytes_accessed=20 << 20, transcendentals=0
        ),
        name="forward_tiles",
    )(rows, cols, srow, scol, sid, meta, scale, adj, *hist, *diff)


def backward_kernel(srow, scol, meta, scale, tiles, *refs):
    parts, outs = refs[:9], refs[9:17]
    grads, acc, sems = refs[17:]
    copies = gather_copies(parts, grads, sems, 0)
    for copy in copies:
        copy.start()
    acc[...] = jnp.zeros_like(acc)
    for copy in copies:
        copy.wait()

    def body(g, carry):
        start = g * GROUP
        products = [
            lax.dot_general(
                tiles[start + u],
                grads[srow[start + u]],
                (((0,), (0,)), ((), ())),
                preferred_element_type=F32,
            )
            * scale[start + u]
            for u in range(GROUP)
        ]
        for u in range(GROUP):
            c = scol[start + u]
            acc[c] = acc[c] + products[u]
        return carry

    lax.fori_loop(0, tiles.shape[0] // GROUP, body, 0)
    xpos, ypos = meta[2], meta[3]
    lanes = acc.shape[2] // 2
    for k in range(4):
        for j in range(4):
            at = (lax.rem(ypos + j, 4) * 4 + lax.rem(xpos + k, 4)) * 4
            block = acc[pl.ds(at, 4)]
            outs[k][4 * j : 4 * j + 4] = block[:, :, :lanes].astype(BF)
            outs[4 + j][4 * k : 4 * k + 4] = block[:, :, lanes:].astype(BF)


def backward_tiles(srow, scol, meta, scale, chosen, parts):
    n, blk, _ = chosen.shape
    half = parts[0].shape[-1]
    return pl.pallas_call(
        backward_kernel,
        out_shape=[jax.ShapeDtypeStruct((16, blk, half // 2), BF)] * 8,
        in_specs=[SMEM] * 4 + [VMEM] + [HBM] * 9,
        out_specs=[VMEM] * 8,
        scratch_shapes=[
            pltpu.VMEM((32, blk, half), BF),
            pltpu.VMEM((64, blk, half), F32),
            pltpu.SemaphoreType.DMA((9,)),
        ],
        compiler_params=pltpu.CompilerParams(vmem_limit_bytes=60 * 1024 * 1024),
        cost_estimate=pl.CostEstimate(
            flops=2 * n * blk * blk * half, bytes_accessed=8 << 20, transcendentals=0
        ),
        name="backward_tiles",
    )(srow, scol, meta, scale, chosen, *parts)


def scatter_both(left, right):
    axes = (("x", "y"), ("y", "x"))
    both = (left, right)
    one = [shift(p[1], a, 1) for p, (a, _) in zip(both, axes)]
    three = [shift(p[3], a, -1) for p, (a, _) in zip(both, axes)]
    two = [left[2], right[2]]
    one[0], one[1], two[0], two[1] = lax.optimization_barrier((one[0], one[1], two[0], two[1]))
    two = [shift(t, a, 2) for t, (a, _) in zip(two, axes)]
    total = [
        p[0].astype(F32) + i.astype(F32) + t.astype(F32) + m.astype(F32)
        for p, i, t, m in zip(both, one, three, two)
    ]
    out = []
    for t, (_, b) in zip(total, axes):
        send = [t[4 * j : 4 * j + 4].astype(BF) for j in (1, 2, 3)]
        got = [shift(p, b, j if j < 3 else -1) for j, p in zip((1, 2, 3), send)]
        out.append(t[:4] + sum(p.astype(F32) for p in got))
    return jnp.concatenate(out, axis=2)


def dense_kernel(core, z, zo, w, wo, d, do, out, dz, wg):
    half = d.shape[1]
    first = core[0] == 0
    zv = z[...]
    pre = jnp.dot(zv, w[...], preferred_element_type=F32)
    pre += jnp.dot(zo[...], wo[...], preferred_element_type=F32)
    inner = 0.7978845608 * (pre + 0.044715 * pre * pre * pre)
    th = jnp.tanh(inner)
    cdf = 0.5 * (1.0 + th)
    act = pre * cdf
    out[...] = jnp.where(first, act[:, :half], act[:, half:]).astype(out.dtype)
    slope = cdf + 0.5 * pre * (1.0 - th * th) * (
        0.7978845608 * (1.0 + 3.0 * 0.044715 * pre * pre)
    )
    mine, other = d[...].astype(F32), do[...].astype(F32)
    cot = jnp.concatenate(
        [jnp.where(first, mine, other), jnp.where(first, other, mine)], axis=1
    )
    g = (cot * slope).astype(BF)
    dz[...] = lax.dot_general(
        g, w[...], (((1,), (1,)), ((), ())), preferred_element_type=F32
    ).astype(BF)
    wg[...] = lax.dot_general(
        zv, g, (((0,), (0,)), ((), ())), preferred_element_type=F32
    ).astype(wg.dtype)


def dense(core, z, zo, w, wo, d, do):
    rows, half = z.shape
    return pl.pallas_call(
        dense_kernel,
        out_shape=[
            jax.ShapeDtypeStruct((rows, half), BF),
            jax.ShapeDtypeStruct((rows, half), BF),
            jax.ShapeDtypeStruct(w.shape, BF),
        ],
        in_specs=[SMEM] + [VMEM] * 6,
        out_specs=[VMEM] * 3,
        compiler_params=pltpu.CompilerParams(vmem_limit_bytes=32 * 1024 * 1024),
        cost_estimate=pl.CostEstimate(
            flops=8 * rows * half * 2 * half, bytes_accessed=2 << 20, transcendentals=rows * half * 2
        ),
        name="dense",
    )(core, z, zo, w, wo, d, do)


def plus(a, b):
    return (a.astype(F32) + b.astype(F32)).astype(BF)


def gather_ring(x):
    blocks = {0: x}
    up = down = x
    for k in (1, 2, 3):
        up, down = shift(up, "z", 1), shift(down, "z", -1)
        blocks[8 - k], blocks[k] = up, down
    half = x.shape[0] // 2
    far_lo = shift(up[:half], "z", 1)
    far_hi = shift(down[half:], "z", -1)
    return [blocks[0], blocks[1], blocks[2], blocks[3], far_lo, far_hi, blocks[5], blocks[6], blocks[7]]


def local(
    fresh, history, adj_val, tile_row, tile_col, tile_count, samp_id, samp_scale, weight, d_out
):
    adj = adj_val[0, 0]
    rows = tile_row[0, 0]
    cols = tile_col[0, 0]
    count = tile_count[0, 0]
    sid = samp_id[0, 0]
    scale = samp_scale[0, 0]
    n_tiles, blk, _ = adj.shape
    half = fresh.shape[1]
    xpos, ypos, zpos = lax.axis_index("x"), lax.axis_index("y"), lax.axis_index("z")
    core = lax.axis_index("core")
    hist_in = history.reshape(4, blk, half)
    diff_in = (fresh.astype(F32) - history.astype(F32)).astype(BF).reshape(4, blk, half)
    hist, diff, tiles = gather_both(hist_in, diff_in, adj)

    xrel = (cols // 4 - xpos) % 4
    yrel = (cols // 16 - ypos) % 4
    hcol = (yrel * 4 + xrel) * 4 + cols % 4
    dcol = (xrel * 4 + yrel) * 4 + cols % 4
    live_row = jnp.where(jnp.arange(n_tiles, dtype=jnp.int32) < count, rows, 32)
    srow = rows[sid]
    meta = jnp.stack([count, zpos, xpos, ypos]).astype(jnp.int32)
    o4a, o4b, o3, o2, o1, o0, m1, m2, m3, chosen = forward_tiles(
        live_row, hcol, srow, dcol[sid], sid, meta, scale, tiles, hist, diff
    )

    up, down = shift(o4a, "z", 1), shift(o4b, "z", -1)
    up = shift(jnp.concatenate([plus(up, o3[:2]), o3[2:]], axis=0), "z", 1)
    down = shift(jnp.concatenate([m3[:2], plus(down, m3[2:])], axis=0), "z", -1)
    up, down = shift(plus(up, o2), "z", 1), shift(plus(down, m2), "z", -1)
    up, down = shift(plus(up, o1), "z", 1), shift(plus(down, m1), "z", -1)
    zval = (up.astype(F32) + down.astype(F32) + o0.astype(F32)).astype(BF)
    zval = zval.reshape(4 * blk, half)

    wother = shift(weight, "core", 1)
    d_other = shift(d_out, "core", 1)
    zother = shift(zval, "core", 1)
    layer_out, dz, wpart = dense(
        core.astype(jnp.int32).reshape(1), zval, zother, weight, wother, d_out, d_other
    )

    parts = gather_ring(dz.reshape(4, blk, half))
    row_rel = ((srow // 4 - zpos) % 8) * 4 + srow % 4
    wide = weight.shape[1]
    wparts = lax.all_to_all(wpart, "z", 0, 0, tiled=True)
    wsum = wparts.reshape(8, half // 8, wide).astype(F32).sum(0).astype(BF)
    wparts = lax.all_to_all(
        jnp.broadcast_to(wsum, (16,) + wsum.shape), ("y", "x"), 0, 0, tiled=True
    )
    wsum = wparts.astype(F32).sum(0).astype(BF)
    wgrad = lax.all_to_all(
        jnp.broadcast_to(wsum, (8,) + wsum.shape), "z", 0, 0, tiled=True
    )
    wgrad = wgrad.reshape(half, wide).astype(F32)
    back = backward_tiles(row_rel, cols[sid], meta, scale, chosen, parts)
    fresh_grad = scatter_both(back[:4], back[4:])
    fresh_grad = fresh_grad.reshape(4 * blk, half)
    return layer_out, wgrad, fresh_grad


def solution(mesh):
    fine = Mesh(mesh.devices.reshape(4, 4, 8, 2), ("y", "x", "z", "core"))
    row = ("y", "x")
    nodes = P(("y", "x", "z"), "core")
    placed = (
        nodes,
        nodes,
        P(row, "z", None, None, None),
        P(row, "z", None),
        P(row, "z", None),
        P(row, "z"),
        P(row, "z", None),
        P(row, "z", None),
        P("core", None),
        nodes,
    )
    return jax.shard_map(
        local,
        mesh=fine,
        in_specs=placed,
        out_specs=(nodes, P("core", None), nodes),
        check_vma=False,
    )
```

```python
import functools
import jax
import jax.numpy as jnp
from jax import lax
from jax.experimental import pallas as pl
from jax.experimental.pallas import tpu as pltpu
from jax.sharding import Mesh, PartitionSpec as P

BF = jnp.bfloat16
F32 = jnp.float32
GROUP = 8
PARTS = 8
VMEM = pl.BlockSpec(memory_space=pltpu.VMEM)
HBM = pl.BlockSpec(memory_space=pl.ANY)
SMEM = pl.BlockSpec(memory_space=pltpu.SMEM)


def shift(x, axis, step):
    n = lax.axis_size(axis)
    return lax.ppermute(x, axis, [(i, (i + step) % n) for i in range(n)])


def join(a, b):
    return jnp.concatenate([a, b], axis=0)


def gather_both(one, two, adj):
    axes = (("x", "y"), ("y", "x"))
    own = (one, two)
    next_ = [shift(v, a, -1) for v, (a, _) in zip(own, axes)]
    prev = [shift(v, a, 1) for v, (a, _) in zip(own, axes)]
    far = [shift(v, a, 2) for v, (a, _) in zip(own, axes)]
    low = [join(v, n) for v, n in zip(own, next_)]
    high = [join(f, p) for f, p in zip(far, prev)]
    low[0], high[0] = lax.optimization_barrier((low[0], high[0]))
    low[1], high[1] = lax.optimization_barrier((low[1], high[1]))
    below_low = [shift(v, b, 1) for v, (_, b) in zip(low, axes)]
    above_high = [shift(v, b, -1) for v, (_, b) in zip(high, axes)]
    late_low, late_high = low, high
    below_low[0], adj = lax.optimization_barrier((below_low[0], adj))
    tiles = load_tiles(adj)
    far_low = [shift(v, b, 1) for v, (_, b) in zip(below_low, axes)]
    far_high = [shift(v, b, -1) for v, (_, b) in zip(above_high, axes)]
    above_low = [shift(v, b, -1) for v, (_, b) in zip(late_low, axes)]
    below_high = [shift(v, b, 1) for v, (_, b) in zip(late_high, axes)]
    return [
        (low[n], high[n], above_low[n], above_high[n], far_low[n], far_high[n], below_low[n], below_high[n])
        for n in range(2)
    ] + [tiles]


def gather_copies(parts, dst, sems, base):
    copies = []
    at = 0
    for n, part in enumerate(parts):
        size = part.shape[0]
        copies.append(pltpu.make_async_copy(part, dst.at[pl.ds(at, size)], sems.at[base + n]))
        at += size
    return copies


def load_kernel(src, dst):
    def move(sem):
        copy = pltpu.make_async_copy(src, dst, sem)
        copy.start()
        copy.wait()

    pl.run_scoped(move, pltpu.SemaphoreType.DMA)


def load_tiles(adj):
    return pl.pallas_call(
        load_kernel,
        out_shape=jax.ShapeDtypeStruct(adj.shape, adj.dtype),
        in_specs=[HBM],
        out_specs=VMEM,
        compiler_params=pltpu.CompilerParams(vmem_limit_bytes=16 * 1024 * 1024),
        cost_estimate=pl.CostEstimate(flops=0, bytes_accessed=8 << 20, transcendentals=0),
        name="load_tiles",
    )(adj)


def forward_kernel(rows, cols, srow, scol, sid, meta, scale, tiles, *refs):
    parts, rest = refs[: 2 * PARTS], refs[2 * PARTS :]
    o4a, o4b, o3, o2, o1, o0, m1, m2, m3, chosen = rest[:10]
    hist, diff, acc, sems = rest[10:]
    count = meta[0]
    zpos = meta[1]
    nodes = gather_copies(parts[:PARTS], hist, sems, 0)
    nodes += gather_copies(parts[PARTS:], diff, sems, PARTS)
    for copy in nodes[:PARTS]:
        copy.start()
    for copy in nodes[PARTS:]:
        copy.start()
    acc[...] = jnp.zeros_like(acc)
    for copy in nodes[:PARTS]:
        copy.wait()
    groups = (count + GROUP - 1) // GROUP

    def body(g, carry):
        start = g * GROUP
        products = [
            jnp.dot(tiles[start + u], hist[cols[start + u]], preferred_element_type=F32)
            for u in range(GROUP)
        ]
        for u in range(GROUP):
            r = rows[start + u]
            acc[r] = acc[r] + products[u]
        return carry

    lax.fori_loop(0, groups, body, 0)
    for copy in nodes[PARTS:]:
        copy.wait()

    def sampled(g, carry):
        start = g * GROUP
        for u in range(GROUP):
            chosen[start + u] = tiles[sid[start + u]]
        products = [
            jnp.dot(
                tiles[sid[start + u]], diff[scol[start + u]], preferred_element_type=F32
            )
            * scale[start + u]
            for u in range(GROUP)
        ]
        for u in range(GROUP):
            r = srow[start + u]
            acc[r] = acc[r] + products[u]
        return carry

    lax.fori_loop(0, sid.shape[0] // GROUP, sampled, 0)

    def put(out, k, lo, size):
        start = lax.rem(zpos + k, 8) * 4 + lo
        out[...] = acc[pl.ds(start, size)].astype(out.dtype)

    put(o4a, 4, 0, 2)
    put(o4b, 4, 2, 2)
    for out, k in ((o3, 3), (o2, 2), (o1, 1), (o0, 0), (m1, 7), (m2, 6), (m3, 5)):
        put(out, k, 0, 4)


def forward_tiles(rows, cols, srow, scol, sid, meta, scale, adj, hist, diff):
    n_tiles, blk, _ = adj.shape
    half = hist[0].shape[-1]
    whole = jax.ShapeDtypeStruct((4, blk, half), BF)
    part = jax.ShapeDtypeStruct((2, blk, half), BF)
    chosen = jax.ShapeDtypeStruct((sid.shape[0], blk, blk), BF)
    return pl.pallas_call(
        forward_kernel,
        out_shape=[part, part] + [whole] * 7 + [chosen],
        in_specs=[SMEM] * 7 + [VMEM] + [HBM] * (2 * PARTS),
        out_specs=[VMEM] * 10,
        scratch_shapes=[
            pltpu.VMEM((64, blk, half), BF),
            pltpu.VMEM((64, blk, half), BF),
            pltpu.VMEM((33, blk, half), F32),
            pltpu.SemaphoreType.DMA((2 * PARTS,)),
        ],
        compiler_params=pltpu.CompilerParams(vmem_limit_bytes=26 * 1024 * 1024),
        cost_estimate=pl.CostEstimate(
            flops=2 * 304 * blk * blk * half, bytes_accessed=20 << 20, transcendentals=0
        ),
        name="forward_tiles",
    )(rows, cols, srow, scol, sid, meta, scale, adj, *hist, *diff)


def backward_kernel(srow, scol, meta, scale, tiles, *refs):
    parts, outs = refs[:9], refs[9:17]
    grads, acc, sems = refs[17:]
    copies = gather_copies(parts, grads, sems, 0)
    for copy in copies:
        copy.start()
    acc[...] = jnp.zeros_like(acc)
    for copy in copies:
        copy.wait()

    def body(g, carry):
        start = g * GROUP
        products = [
            lax.dot_general(
                tiles[start + u],
                grads[srow[start + u]],
                (((0,), (0,)), ((), ())),
                preferred_element_type=F32,
            )
            * scale[start + u]
            for u in range(GROUP)
        ]
        for u in range(GROUP):
            c = scol[start + u]
            acc[c] = acc[c] + products[u]
        return carry

    lax.fori_loop(0, tiles.shape[0] // GROUP, body, 0)
    xpos, ypos = meta[2], meta[3]
    lanes = acc.shape[2] // 2
    for k in range(4):
        for j in range(4):
            at = (lax.rem(ypos + j, 4) * 4 + lax.rem(xpos + k, 4)) * 4
            block = acc[pl.ds(at, 4)]
            outs[k][4 * j : 4 * j + 4] = block[:, :, :lanes].astype(BF)
            outs[4 + j][4 * k : 4 * k + 4] = block[:, :, lanes:].astype(BF)


def backward_tiles(srow, scol, meta, scale, chosen, parts):
    n, blk, _ = chosen.shape
    half = parts[0].shape[-1]
    return pl.pallas_call(
        backward_kernel,
        out_shape=[jax.ShapeDtypeStruct((16, blk, half // 2), BF)] * 8,
        in_specs=[SMEM] * 4 + [VMEM] + [HBM] * 9,
        out_specs=[VMEM] * 8,
        scratch_shapes=[
            pltpu.VMEM((32, blk, half), BF),
            pltpu.VMEM((64, blk, half), F32),
            pltpu.SemaphoreType.DMA((9,)),
        ],
        compiler_params=pltpu.CompilerParams(vmem_limit_bytes=60 * 1024 * 1024),
        cost_estimate=pl.CostEstimate(
            flops=2 * n * blk * blk * half, bytes_accessed=8 << 20, transcendentals=0
        ),
        name="backward_tiles",
    )(srow, scol, meta, scale, chosen, *parts)


def scatter_both(left, right):
    axes = (("x", "y"), ("y", "x"))
    both = (left, right)
    one = [shift(p[1], a, 1) for p, (a, _) in zip(both, axes)]
    three = [shift(p[3], a, -1) for p, (a, _) in zip(both, axes)]
    two = [left[2], right[2]]
    one[0], one[1], two[0], two[1] = lax.optimization_barrier((one[0], one[1], two[0], two[1]))
    two = [shift(t, a, 2) for t, (a, _) in zip(two, axes)]
    total = [
        p[0].astype(F32) + i.astype(F32) + t.astype(F32) + m.astype(F32)
        for p, i, t, m in zip(both, one, three, two)
    ]
    out = []
    for t, (_, b) in zip(total, axes):
        send = [t[4 * j : 4 * j + 4].astype(BF) for j in (1, 2, 3)]
        got = [shift(p, b, j if j < 3 else -1) for j, p in zip((1, 2, 3), send)]
        out.append(t[:4] + sum(p.astype(F32) for p in got))
    return jnp.concatenate(out, axis=2)


def dense_kernel(core, z, zo, w, wo, d, do, out, dz, wg):
    half = d.shape[1]
    first = core[0] == 0
    zv = z[...]
    pre = jnp.dot(zv, w[...], preferred_element_type=F32)
    pre += jnp.dot(zo[...], wo[...], preferred_element_type=F32)
    inner = 0.7978845608 * (pre + 0.044715 * pre * pre * pre)
    th = jnp.tanh(inner)
    cdf = 0.5 * (1.0 + th)
    act = pre * cdf
    out[...] = jnp.where(first, act[:, :half], act[:, half:]).astype(out.dtype)
    slope = cdf + 0.5 * pre * (1.0 - th * th) * (
        0.7978845608 * (1.0 + 3.0 * 0.044715 * pre * pre)
    )
    mine, other = d[...].astype(F32), do[...].astype(F32)
    cot = jnp.concatenate(
        [jnp.where(first, mine, other), jnp.where(first, other, mine)], axis=1
    )
    g = (cot * slope).astype(BF)
    dz[...] = lax.dot_general(
        g, w[...], (((1,), (1,)), ((), ())), preferred_element_type=F32
    ).astype(BF)
    wg[...] = lax.dot_general(
        zv, g, (((0,), (0,)), ((), ())), preferred_element_type=F32
    ).astype(wg.dtype)


def dense(core, z, zo, w, wo, d, do):
    rows, half = z.shape
    return pl.pallas_call(
        dense_kernel,
        out_shape=[
            jax.ShapeDtypeStruct((rows, half), BF),
            jax.ShapeDtypeStruct((rows, half), BF),
            jax.ShapeDtypeStruct(w.shape, BF),
        ],
        in_specs=[SMEM] + [VMEM] * 6,
        out_specs=[VMEM] * 3,
        compiler_params=pltpu.CompilerParams(vmem_limit_bytes=32 * 1024 * 1024),
        cost_estimate=pl.CostEstimate(
            flops=8 * rows * half * 2 * half, bytes_accessed=2 << 20, transcendentals=rows * half * 2
        ),
        name="dense",
    )(core, z, zo, w, wo, d, do)


def plus(a, b):
    return (a.astype(F32) + b.astype(F32)).astype(BF)


def gather_ring(x):
    blocks = {0: x}
    up = down = x
    for k in (1, 2, 3):
        up, down = shift(up, "z", 1), shift(down, "z", -1)
        blocks[8 - k], blocks[k] = up, down
    half = x.shape[0] // 2
    far_lo = shift(up[:half], "z", 1)
    far_hi = shift(down[half:], "z", -1)
    return [blocks[0], blocks[1], blocks[2], blocks[3], far_lo, far_hi, blocks[5], blocks[6], blocks[7]]


def local(
    fresh, history, adj_val, tile_row, tile_col, tile_count, samp_id, samp_scale, weight, d_out
):
    adj = adj_val[0, 0]
    rows = tile_row[0, 0]
    cols = tile_col[0, 0]
    count = tile_count[0, 0]
    sid = samp_id[0, 0]
    scale = samp_scale[0, 0]
    n_tiles, blk, _ = adj.shape
    half = fresh.shape[1]
    xpos, ypos, zpos = lax.axis_index("x"), lax.axis_index("y"), lax.axis_index("z")
    core = lax.axis_index("core")
    hist_in = history.reshape(4, blk, half)
    diff_in = (fresh.astype(F32) - history.astype(F32)).astype(BF).reshape(4, blk, half)
    hist, diff, tiles = gather_both(hist_in, diff_in, adj)

    xrel = (cols // 4 - xpos) % 4
    yrel = (cols // 16 - ypos) % 4
    hcol = (yrel * 4 + xrel) * 4 + cols % 4
    dcol = (xrel * 4 + yrel) * 4 + cols % 4
    live_row = jnp.where(jnp.arange(n_tiles, dtype=jnp.int32) < count, rows, 32)
    srow = rows[sid]
    meta = jnp.stack([count, zpos, xpos, ypos]).astype(jnp.int32)
    o4a, o4b, o3, o2, o1, o0, m1, m2, m3, chosen = forward_tiles(
        live_row, hcol, srow, dcol[sid], sid, meta, scale, tiles, hist, diff
    )

    up, down = shift(o4a, "z", 1), shift(o4b, "z", -1)
    up = shift(jnp.concatenate([plus(up, o3[:2]), o3[2:]], axis=0), "z", 1)
    down = shift(jnp.concatenate([m3[:2], plus(down, m3[2:])], axis=0), "z", -1)
    up, down = shift(plus(up, o2), "z", 1), shift(plus(down, m2), "z", -1)
    up, down = shift(plus(up, o1), "z", 1), shift(plus(down, m1), "z", -1)
    zval = (up.astype(F32) + down.astype(F32) + o0.astype(F32)).astype(BF)
    zval = zval.reshape(4 * blk, half)

    wother = shift(weight, "core", 1)
    d_other = shift(d_out, "core", 1)
    zother = shift(zval, "core", 1)
    layer_out, dz, wpart = dense(
        core.astype(jnp.int32).reshape(1), zval, zother, weight, wother, d_out, d_other
    )

    parts = gather_ring(dz.reshape(4, blk, half))
    row_rel = ((srow // 4 - zpos) % 8) * 4 + srow % 4
    wide = weight.shape[1]
    wparts = lax.all_to_all(wpart, "z", 0, 0, tiled=True)
    wsum = wparts.reshape(8, half // 8, wide).astype(F32).sum(0).astype(BF)
    wparts = lax.all_to_all(
        jnp.broadcast_to(wsum, (16,) + wsum.shape), ("y", "x"), 0, 0, tiled=True
    )
    wsum = wparts.astype(F32).sum(0).astype(BF)
    wgrad = lax.all_to_all(
        jnp.broadcast_to(wsum, (8,) + wsum.shape), "z", 0, 0, tiled=True
    )
    wgrad = wgrad.reshape(half, wide).astype(F32)
    back = backward_tiles(row_rel, cols[sid], meta, scale, chosen, parts)
    fresh_grad = scatter_both(back[:4], back[4:])
    fresh_grad = fresh_grad.reshape(4 * blk, half)
    return layer_out, wgrad, fresh_grad


def solution(mesh):
    fine = Mesh(mesh.devices.reshape(4, 4, 8, 2), ("y", "x", "z", "core"))
    row = ("y", "x")
    nodes = P(("y", "x", "z"), "core")
    placed = (
        nodes,
        nodes,
        P(row, "z", None, None, None),
        P(row, "z", None),
        P(row, "z", None),
        P(row, "z"),
        P(row, "z", None),
        P(row, "z", None),
        P("core", None),
        nodes,
    )
    return jax.shard_map(
        local,
        mesh=fine,
        in_specs=placed,
        out_specs=(nodes, P("core", None), nodes),
        check_vma=False,
    )
```

```python
import functools
import jax
import jax.numpy as jnp
from jax import lax
from jax.experimental import pallas as pl
from jax.experimental.pallas import tpu as pltpu
from jax.sharding import Mesh, PartitionSpec as P

BF = jnp.bfloat16
F32 = jnp.float32
GROUP = 16
PARTS = 8
VMEM = pl.BlockSpec(memory_space=pltpu.VMEM)
HBM = pl.BlockSpec(memory_space=pl.ANY)
SMEM = pl.BlockSpec(memory_space=pltpu.SMEM)


def shift(x, axis, step):
    n = lax.axis_size(axis)
    return lax.ppermute(x, axis, [(i, (i + step) % n) for i in range(n)])


def join(a, b):
    return jnp.concatenate([a, b], axis=0)


def gather_both(one, two, adj):
    axes = (("x", "y"), ("y", "x"))
    own = (one, two)
    next_ = [shift(v, a, -1) for v, (a, _) in zip(own, axes)]
    prev = [shift(v, a, 1) for v, (a, _) in zip(own, axes)]
    far = [shift(v, a, 2) for v, (a, _) in zip(own, axes)]
    low = [join(v, n) for v, n in zip(own, next_)]
    high = [join(f, p) for f, p in zip(far, prev)]
    low[0], high[0] = lax.optimization_barrier((low[0], high[0]))
    low[1], high[1] = lax.optimization_barrier((low[1], high[1]))
    below_low = [shift(v, b, 1) for v, (_, b) in zip(low, axes)]
    above_high = [shift(v, b, -1) for v, (_, b) in zip(high, axes)]
    late_low, late_high = low, high
    below_low[0], adj = lax.optimization_barrier((below_low[0], adj))
    tiles = load_tiles(adj)
    far_low = [shift(v, b, 1) for v, (_, b) in zip(below_low, axes)]
    far_high = [shift(v, b, -1) for v, (_, b) in zip(above_high, axes)]
    above_low = [shift(v, b, -1) for v, (_, b) in zip(late_low, axes)]
    below_high = [shift(v, b, 1) for v, (_, b) in zip(late_high, axes)]
    return [
        (low[n], high[n], above_low[n], above_high[n], far_low[n], far_high[n], below_low[n], below_high[n])
        for n in range(2)
    ] + [tiles]


def gather_copies(parts, dst, sems, base):
    copies = []
    at = 0
    for n, part in enumerate(parts):
        size = part.shape[0]
        copies.append(pltpu.make_async_copy(part, dst.at[pl.ds(at, size)], sems.at[base + n]))
        at += size
    return copies


def load_kernel(src, dst):
    def move(sem):
        copy = pltpu.make_async_copy(src, dst, sem)
        copy.start()
        copy.wait()

    pl.run_scoped(move, pltpu.SemaphoreType.DMA)


def load_tiles(adj):
    return pl.pallas_call(
        load_kernel,
        out_shape=jax.ShapeDtypeStruct(adj.shape, adj.dtype),
        in_specs=[HBM],
        out_specs=VMEM,
        compiler_params=pltpu.CompilerParams(vmem_limit_bytes=16 * 1024 * 1024),
        cost_estimate=pl.CostEstimate(flops=0, bytes_accessed=8 << 20, transcendentals=0),
        name="load_tiles",
    )(adj)


def forward_kernel(rows, cols, srow, scol, sid, meta, scale, tiles, *refs):
    parts, rest = refs[: 2 * PARTS], refs[2 * PARTS :]
    o4a, o4b, o3, o2, o1, o0, m1, m2, m3, chosen = rest[:10]
    hist, diff, acc, sems = rest[10:]
    count = meta[0]
    zpos = meta[1]
    nodes = gather_copies(parts[:PARTS], hist, sems, 0)
    nodes += gather_copies(parts[PARTS:], diff, sems, PARTS)
    for copy in nodes[:PARTS]:
        copy.start()
    for copy in nodes[PARTS:]:
        copy.start()
    acc[...] = jnp.zeros_like(acc)
    for copy in nodes[:PARTS]:
        copy.wait()
    groups = (count + GROUP - 1) // GROUP

    def body(g, carry):
        start = g * GROUP
        products = [
            jnp.dot(tiles[start + u], hist[cols[start + u]], preferred_element_type=F32)
            for u in range(GROUP)
        ]
        for u in range(GROUP):
            r = rows[start + u]
            acc[r] = acc[r] + products[u]
        return carry

    lax.fori_loop(0, groups, body, 0)
    for copy in nodes[PARTS:]:
        copy.wait()

    def sampled(g, carry):
        start = g * GROUP
        for u in range(GROUP):
            chosen[start + u] = tiles[sid[start + u]]
        products = [
            jnp.dot(
                tiles[sid[start + u]], diff[scol[start + u]], preferred_element_type=F32
            )
            * scale[start + u]
            for u in range(GROUP)
        ]
        for u in range(GROUP):
            r = srow[start + u]
            acc[r] = acc[r] + products[u]
        return carry

    lax.fori_loop(0, sid.shape[0] // GROUP, sampled, 0)

    def put(out, k, lo, size):
        start = lax.rem(zpos + k, 8) * 4 + lo
        out[...] = acc[pl.ds(start, size)].astype(out.dtype)

    put(o4a, 4, 0, 2)
    put(o4b, 4, 2, 2)
    for out, k in ((o3, 3), (o2, 2), (o1, 1), (o0, 0), (m1, 7), (m2, 6), (m3, 5)):
        put(out, k, 0, 4)


def forward_tiles(rows, cols, srow, scol, sid, meta, scale, adj, hist, diff):
    n_tiles, blk, _ = adj.shape
    half = hist[0].shape[-1]
    whole = jax.ShapeDtypeStruct((4, blk, half), BF)
    part = jax.ShapeDtypeStruct((2, blk, half), BF)
    chosen = jax.ShapeDtypeStruct((sid.shape[0], blk, blk), BF)
    return pl.pallas_call(
        forward_kernel,
        out_shape=[part, part] + [whole] * 7 + [chosen],
        in_specs=[SMEM] * 7 + [VMEM] + [HBM] * (2 * PARTS),
        out_specs=[VMEM] * 10,
        scratch_shapes=[
            pltpu.VMEM((64, blk, half), BF),
            pltpu.VMEM((64, blk, half), BF),
            pltpu.VMEM((33, blk, half), F32),
            pltpu.SemaphoreType.DMA((2 * PARTS,)),
        ],
        compiler_params=pltpu.CompilerParams(vmem_limit_bytes=26 * 1024 * 1024),
        cost_estimate=pl.CostEstimate(
            flops=2 * 304 * blk * blk * half, bytes_accessed=20 << 20, transcendentals=0
        ),
        name="forward_tiles",
    )(rows, cols, srow, scol, sid, meta, scale, adj, *hist, *diff)


def backward_kernel(srow, scol, meta, scale, tiles, *refs):
    parts, outs = refs[:9], refs[9:17]
    grads, acc, sems = refs[17:]
    copies = gather_copies(parts, grads, sems, 0)
    for copy in copies:
        copy.start()
    acc[...] = jnp.zeros_like(acc)
    for copy in copies:
        copy.wait()

    def body(g, carry):
        start = g * GROUP
        products = [
            lax.dot_general(
                tiles[start + u],
                grads[srow[start + u]],
                (((0,), (0,)), ((), ())),
                preferred_element_type=F32,
            )
            * scale[start + u]
            for u in range(GROUP)
        ]
        for u in range(GROUP):
            c = scol[start + u]
            acc[c] = acc[c] + products[u]
        return carry

    lax.fori_loop(0, tiles.shape[0] // GROUP, body, 0)
    xpos, ypos = meta[2], meta[3]
    lanes = acc.shape[2] // 2
    for k in range(4):
        for j in range(4):
            at = (lax.rem(ypos + j, 4) * 4 + lax.rem(xpos + k, 4)) * 4
            block = acc[pl.ds(at, 4)]
            outs[k][4 * j : 4 * j + 4] = block[:, :, :lanes].astype(BF)
            outs[4 + j][4 * k : 4 * k + 4] = block[:, :, lanes:].astype(BF)


def backward_tiles(srow, scol, meta, scale, chosen, parts):
    n, blk, _ = chosen.shape
    half = parts[0].shape[-1]
    return pl.pallas_call(
        backward_kernel,
        out_shape=[jax.ShapeDtypeStruct((16, blk, half // 2), BF)] * 8,
        in_specs=[SMEM] * 4 + [VMEM] + [HBM] * 9,
        out_specs=[VMEM] * 8,
        scratch_shapes=[
            pltpu.VMEM((32, blk, half), BF),
            pltpu.VMEM((64, blk, half), F32),
            pltpu.SemaphoreType.DMA((9,)),
        ],
        compiler_params=pltpu.CompilerParams(vmem_limit_bytes=60 * 1024 * 1024),
        cost_estimate=pl.CostEstimate(
            flops=2 * n * blk * blk * half, bytes_accessed=8 << 20, transcendentals=0
        ),
        name="backward_tiles",
    )(srow, scol, meta, scale, chosen, *parts)


def scatter_both(left, right):
    axes = (("x", "y"), ("y", "x"))
    both = (left, right)
    one = [shift(p[1], a, 1) for p, (a, _) in zip(both, axes)]
    three = [shift(p[3], a, -1) for p, (a, _) in zip(both, axes)]
    two = [left[2], right[2]]
    two = [shift(t, a, 2) for t, (a, _) in zip(two, axes)]
    total = [
        p[0].astype(F32) + i.astype(F32) + t.astype(F32) + m.astype(F32)
        for p, i, t, m in zip(both, one, three, two)
    ]
    out = []
    for t, (_, b) in zip(total, axes):
        send = [t[4 * j : 4 * j + 4].astype(BF) for j in (1, 2, 3)]
        got = [shift(p, b, j if j < 3 else -1) for j, p in zip((1, 2, 3), send)]
        out.append(t[:4] + sum(p.astype(F32) for p in got))
    return jnp.concatenate(out, axis=2)


def dense_kernel(core, z, zo, w, wo, d, do, out, dz, wg):
    half = d.shape[1]
    first = core[0] == 0
    zv = z[...]
    pre = jnp.dot(zv, w[...], preferred_element_type=F32)
    pre += jnp.dot(zo[...], wo[...], preferred_element_type=F32)
    inner = 0.7978845608 * (pre + 0.044715 * pre * pre * pre)
    th = jnp.tanh(inner)
    cdf = 0.5 * (1.0 + th)
    act = pre * cdf
    out[...] = jnp.where(first, act[:, :half], act[:, half:]).astype(out.dtype)
    slope = cdf + 0.5 * pre * (1.0 - th * th) * (
        0.7978845608 * (1.0 + 3.0 * 0.044715 * pre * pre)
    )
    mine, other = d[...].astype(F32), do[...].astype(F32)
    cot = jnp.concatenate(
        [jnp.where(first, mine, other), jnp.where(first, other, mine)], axis=1
    )
    g = (cot * slope).astype(BF)
    dz[...] = lax.dot_general(
        g, w[...], (((1,), (1,)), ((), ())), preferred_element_type=F32
    ).astype(BF)
    wg[...] = lax.dot_general(
        zv, g, (((0,), (0,)), ((), ())), preferred_element_type=F32
    ).astype(wg.dtype)


def dense(core, z, zo, w, wo, d, do):
    rows, half = z.shape
    return pl.pallas_call(
        dense_kernel,
        out_shape=[
            jax.ShapeDtypeStruct((rows, half), BF),
            jax.ShapeDtypeStruct((rows, half), BF),
            jax.ShapeDtypeStruct(w.shape, BF),
        ],
        in_specs=[SMEM] + [VMEM] * 6,
        out_specs=[VMEM] * 3,
        compiler_params=pltpu.CompilerParams(vmem_limit_bytes=32 * 1024 * 1024),
        cost_estimate=pl.CostEstimate(
            flops=8 * rows * half * 2 * half, bytes_accessed=2 << 20, transcendentals=rows * half * 2
        ),
        name="dense",
    )(core, z, zo, w, wo, d, do)


def plus(a, b):
    return (a.astype(F32) + b.astype(F32)).astype(BF)


def gather_ring(x):
    blocks = {0: x}
    up = down = x
    for k in (1, 2, 3):
        up, down = shift(up, "z", 1), shift(down, "z", -1)
        blocks[8 - k], blocks[k] = up, down
    half = x.shape[0] // 2
    far_lo = shift(up[:half], "z", 1)
    far_hi = shift(down[half:], "z", -1)
    return [blocks[0], blocks[1], blocks[2], blocks[3], far_lo, far_hi, blocks[5], blocks[6], blocks[7]]


def local(
    fresh, history, adj_val, tile_row, tile_col, tile_count, samp_id, samp_scale, weight, d_out
):
    adj = adj_val[0, 0]
    rows = tile_row[0, 0]
    cols = tile_col[0, 0]
    count = tile_count[0, 0]
    sid = samp_id[0, 0]
    scale = samp_scale[0, 0]
    n_tiles, blk, _ = adj.shape
    half = fresh.shape[1]
    xpos, ypos, zpos = lax.axis_index("x"), lax.axis_index("y"), lax.axis_index("z")
    core = lax.axis_index("core")
    hist_in = history.reshape(4, blk, half)
    diff_in = (fresh.astype(F32) - history.astype(F32)).astype(BF).reshape(4, blk, half)
    hist, diff, tiles = gather_both(hist_in, diff_in, adj)

    xrel = (cols // 4 - xpos) % 4
    yrel = (cols // 16 - ypos) % 4
    hcol = (yrel * 4 + xrel) * 4 + cols % 4
    dcol = (xrel * 4 + yrel) * 4 + cols % 4
    live_row = jnp.where(jnp.arange(n_tiles, dtype=jnp.int32) < count, rows, 32)
    srow = rows[sid]
    meta = jnp.stack([count, zpos, xpos, ypos]).astype(jnp.int32)
    o4a, o4b, o3, o2, o1, o0, m1, m2, m3, chosen = forward_tiles(
        live_row, hcol, srow, dcol[sid], sid, meta, scale, tiles, hist, diff
    )

    up, down = shift(o4a, "z", 1), shift(o4b, "z", -1)
    up = shift(jnp.concatenate([plus(up, o3[:2]), o3[2:]], axis=0), "z", 1)
    down = shift(jnp.concatenate([m3[:2], plus(down, m3[2:])], axis=0), "z", -1)
    up, down = shift(plus(up, o2), "z", 1), shift(plus(down, m2), "z", -1)
    up, down = shift(plus(up, o1), "z", 1), shift(plus(down, m1), "z", -1)
    zval = (up.astype(F32) + down.astype(F32) + o0.astype(F32)).astype(BF)
    zval = zval.reshape(4 * blk, half)

    wother = shift(weight, "core", 1)
    d_other = shift(d_out, "core", 1)
    zother = shift(zval, "core", 1)
    layer_out, dz, wpart = dense(
        core.astype(jnp.int32).reshape(1), zval, zother, weight, wother, d_out, d_other
    )

    parts = gather_ring(dz.reshape(4, blk, half))
    row_rel = ((srow // 4 - zpos) % 8) * 4 + srow % 4
    wide = weight.shape[1]
    wparts = lax.all_to_all(wpart, "z", 0, 0, tiled=True)
    wsum = wparts.reshape(8, half // 8, wide).astype(F32).sum(0).astype(BF)
    wparts = lax.all_to_all(
        jnp.broadcast_to(wsum, (16,) + wsum.shape), ("y", "x"), 0, 0, tiled=True
    )
    wsum = wparts.astype(F32).sum(0).astype(BF)
    wgrad = lax.all_to_all(
        jnp.broadcast_to(wsum, (8,) + wsum.shape), "z", 0, 0, tiled=True
    )
    wgrad = wgrad.reshape(half, wide).astype(F32)
    back = backward_tiles(row_rel, cols[sid], meta, scale, chosen, parts)
    fresh_grad = scatter_both(back[:4], back[4:])
    fresh_grad = fresh_grad.reshape(4 * blk, half)
    return layer_out, wgrad, fresh_grad


def solution(mesh):
    fine = Mesh(mesh.devices.reshape(4, 4, 8, 2), ("y", "x", "z", "core"))
    row = ("y", "x")
    nodes = P(("y", "x", "z"), "core")
    placed = (
        nodes,
        nodes,
        P(row, "z", None, None, None),
        P(row, "z", None),
        P(row, "z", None),
        P(row, "z"),
        P(row, "z", None),
        P(row, "z", None),
        P("core", None),
        nodes,
    )
    return jax.shard_map(
        local,
        mesh=fine,
        in_specs=placed,
        out_specs=(nodes, P("core", None), nodes),
        check_vma=False,
    )
```
